1024 devices in a mesh: dp: 16 (over y, x), mp: 64 (over z, core).
Axes of the slice: x: 4, y: 4, z: 32, core: 2. Of those that a mesh axis runs over, the one named last changes fastest.
Arguments:
- acts: bfloat16 [64, 8192, 512], P('mp', 'dp'), may hold values from -6 to 6
- outgrads: bfloat16 [64, 8192, 512], P('mp', 'dp'), may hold values from -6 to 6
- grad: bfloat16 [64, 512, 512], P(None, None, 'mp'), may hold values from -6 to 6
- owners: int32 [64, 2], P('mp'), may hold values from 0 to 15, all different within a row
Outputs:
- kept_roots: float32 [16, 64, 2, 512, 512], P('dp', 'mp')
- precond: float32 [64, 512, 512], P(None, None, 'mp')
The draws below stay inside these ranges and needn't reach their ends.
Inputs may be any that keep to these rules, and one draw needn't show every extreme that they name: The two owners of a tile are different; every dp index owns some root.
All inputs are finite; a program needn't handle non-finite values.
Results may differ from the reference program's by a relative error of at most 0.006.
Values may be sent and summed in bfloat16 or wider, within the bound.
No kernel may reach another device: no remote copies, remote signals or barrier semaphores. Data moves between devices by JAX's collectives and lax.ppermute only.
A program may use at most 32 MiB of HBM per device.

```python
import jax
import jax.numpy as jnp
from jax import lax

B = 512
ITERS = 2
TILES = 64
TOKENS = 8192
N_DP = 16


def level_of(key, dims, shards, least, top_value):
    def one(dim, parts):
        heights = jax.random.uniform(jax.random.fold_in(jax.random.fold_in(key, 6), dim), (parts,), jnp.float32, least / len(shards), top_value / len(shards))
        return jnp.repeat(jnp.exp(heights), dims[dim] // parts).reshape((-1,) + (1,) * (len(dims) - dim - 1))

    loudness = one(*shards[0])
    for cut in shards[1:]:
        loudness = loudness * one(*cut)
    return loudness


def choose_distinct(own_key, rows, number_of, top, lift):
    ranking = jax.random.permutation(jax.random.fold_in(own_key, 1), number_of)
    boost = ranking
    for power in range(3):
        boost = boost * boost // number_of
    boost = boost * lift // number_of
    chance = jax.random.randint(jax.random.fold_in(own_key, 2), (rows, number_of), 0, 4096) + boost
    holders = jax.random.permutation(jax.random.fold_in(own_key, 3), rows)[jnp.arange(number_of) % rows]
    chance = jnp.where(jnp.arange(rows)[:, None] == holders[None, :], 1 << 14, chance)
    score = chance * number_of + jnp.arange(number_of)
    return lax.top_k(score.astype(jnp.int32), top)[1].astype(jnp.int32)


def bell_draw(own_key, extent, scale, most, cuts=(), kind=jnp.bfloat16):
    loudness = level_of(own_key, extent, cuts, -0.22, 0.18) if cuts else 1.0
    entries = jax.random.normal(own_key, extent, jnp.float32) * scale * loudness
    return jnp.minimum(jnp.maximum(entries, -most), most).astype(kind)


def setup_inputs(seed: int = 0) -> dict:
    key_of = jax.random.split(jax.random.key(seed), 5)
    acts = bell_draw(key_of[0], (TILES, TOKENS, B), 1.0, 6.0, ((0, 64), (1, 16)))
    outgrads = bell_draw(key_of[1], (TILES, TOKENS, B), 1.0, 6.0, ((0, 64), (1, 16)))
    grad = bell_draw(key_of[2], (TILES, B, B), 1.0, 6.0, ((2, 64),))
    owners = choose_distinct(key_of[3], TILES, N_DP, 2, 0)
    return dict(acts=acts, outgrads=outgrads, grad=grad, owners=owners)


damping = 0.001

def newton(stat):
    eye = jnp.eye(stat.shape[0], dtype=jnp.float32)
    scale = jnp.sqrt(jnp.sum(stat * stat))
    matrix = stat / scale
    root = eye * scale ** (-0.25)
    for turn in range(ITERS):
        factor = (5.0 * eye - matrix) * 0.25
        root = jnp.dot(root, factor, precision=lax.Precision.HIGHEST)
        if turn + 1 < ITERS:
            square = jnp.dot(factor, factor, precision=lax.Precision.HIGHEST)
            matrix = jnp.dot(square, jnp.dot(square, matrix, precision=lax.Precision.HIGHEST), precision=lax.Precision.HIGHEST)
    return root

def reference(acts, outgrads, grad, owners):
    eye = jnp.eye(B, dtype=jnp.float32)
    ranks = jnp.arange(N_DP, dtype=jnp.int32)

    def per_tile(items):
        left_in, right_in, tile, owner = items
        left = jnp.dot(left_in.T, left_in, preferred_element_type=jnp.float32) / TOKENS + damping * eye
        right = jnp.dot(right_in.T, right_in, preferred_element_type=jnp.float32) / TOKENS + damping * eye
        left_root = newton(left)
        right_root = newton(right)
        roots = jnp.stack([left_root, right_root])
        marks = (ranks[:, None] == owner[None, :]).astype(jnp.float32)
        kept = marks[:, :, None, None] * roots[None]
        half = jnp.dot(left_root.astype(jnp.bfloat16), tile, preferred_element_type=jnp.float32).astype(jnp.bfloat16)
        mixed = jnp.dot(half, right_root.astype(jnp.bfloat16), preferred_element_type=jnp.float32)
        return (kept, mixed)
    kept, precond = lax.map(per_tile, (acts, outgrads, grad, owners))
    return (jnp.transpose(kept, (1, 0, 2, 3, 4)), precond)
```

```python
import functools

import jax
import jax.numpy as jnp
from jax import lax
from jax.experimental import pallas as pl
from jax.experimental.pallas import tpu as pltpu
from jax.sharding import Mesh, PartitionSpec as P

damping = 0.001
SIDE = 128
LIMIT = 48 * 1024 * 1024


def blocks(width):
    n = width // SIDE
    return [(i, j) for i in range(n) for j in range(i, n)]


def gram_kernel(acts_ref, outs_ref, packed_ref, held_ref, sems):
    tokens, width = acts_ref.shape[1:]
    places = blocks(width)
    wide = 2 * SIDE
    copies = []
    for which, ref in enumerate((acts_ref, outs_ref)):
        for part in range(2):
            span = pl.ds(part * (tokens // 2), tokens // 2)
            copies.append(pltpu.make_async_copy(ref.at[0, span], held_ref.at[which, span], sems.at[which, part]))
            copies[-1].start()
    for which in range(2):
        base = which * len(places)
        copies[2 * which].wait()
        copies[2 * which + 1].wait()
        for i in range(0, width, wide):
            left = held_ref[which, :, i : i + wide]
            part = lax.dot_general(
                left, held_ref[which, :, i:], (((0,), (0,)), ((), ())), preferred_element_type=jnp.float32
            )
            for spot, (r, c) in enumerate(places):
                if i <= r * SIDE < i + wide:
                    row, col = r * SIDE - i, c * SIDE - i
                    packed_ref[pl.ds((base + spot) * SIDE, SIDE), :] = part[
                        row : row + SIDE, col : col + SIDE
                    ].astype(packed_ref.dtype)


def sum_kernel(total_tokens, parts_ref, shards_ref, copies_ref):
    count, rows = parts_ref.shape[:2]
    tall, width = shards_ref.shape[1:]
    for tile in range(2):
        total = parts_ref[tile].astype(jnp.float32)
        for g in range(2 + tile, count, 2):
            total = total + parts_ref[g].astype(jnp.float32)
        total = (total / total_tokens).astype(copies_ref.dtype)
        for g in range(tile, count, 2):
            copies_ref[g, :rows] = total
            for lane in range(width // SIDE):
                copies_ref[g, pl.ds(rows + lane * tall, tall)] = shards_ref[tile, :, lane * SIDE : (lane + 1) * SIDE]


def mm(a, b):
    return jnp.dot(a.astype(jnp.bfloat16), b.astype(jnp.bfloat16), preferred_element_type=jnp.float32)


def diag(width):
    rows = lax.broadcasted_iota(jnp.int32, (width, width), 0)
    cols = lax.broadcasted_iota(jnp.int32, (width, width), 1)
    return rows == cols


def root_kernel(coord_ref, mixed_ref, left_ref, right_ref, piece_ref, stat_ref, tile_ref):
    width = stat_ref.shape[0]
    places = blocks(width)
    on_diag = diag(width)
    for which, root_ref in enumerate((left_ref, right_ref)):
        base = which * len(places)
        share = 2 * len(places) * SIDE // mixed_ref.shape[0]
        for spot, (r, c) in enumerate(places):
            start, stop, pieces = (base + spot) * SIDE, (base + spot + 1) * SIDE, []
            while start < stop:
                size = min(stop, (start // share + 1) * share) - start
                pieces.append(mixed_ref[start // share, pl.ds(start % share, size)])
                start += size
            block = jnp.concatenate(pieces, axis=0).astype(jnp.float32)
            stat_ref[pl.ds(r * SIDE, SIDE), pl.ds(c * SIDE, SIDE)] = block
            if r != c:
                stat_ref[pl.ds(c * SIDE, SIDE), pl.ds(r * SIDE, SIDE)] = block.T
        stat = stat_ref[...] + jnp.where(on_diag, damping, 0.0)
        squares = jnp.sum(jnp.sum(stat * stat, axis=0, keepdims=True), axis=1, keepdims=True)
        inv_scale = 1.0 / jnp.sqrt(squares)
        matrix = stat * inv_scale
        low = matrix.astype(jnp.bfloat16)
        square = mm(low, low)
        shift = square * 0.0625 - matrix * 0.625
        shift_low = shift.astype(jnp.bfloat16)
        quart = mm(shift_low, shift_low) + 3.125 * shift + jnp.where(on_diag, 625.0 / 256.0, 0.0)
        lead = matrix * 1.25 - square * 0.25
        tail = mm(lead, quart)
        factor = jnp.sqrt(jnp.sqrt(inv_scale))
        root_ref[...] = factor * (jnp.where(on_diag, 1.5625, 0.0) - 0.3125 * matrix - 0.25 * tail)

    me, plane = coord_ref[0], coord_ref[1]
    count, planes, tall = mixed_ref.shape[0], mixed_ref.shape[0], 16
    side = tall // 2
    for d in range(count // 2):
        for lane in range(width // SIDE):
            low_rows = pl.ds(share + lane * tall, tall)
            even, odd = mixed_ref[2 * d, low_rows].astype(jnp.float32), mixed_ref[2 * d + 1, low_rows].astype(jnp.float32)
            for j in range(2):
                source = lax.rem(plane - shift_of(d, j) + 2 * planes, planes)
                both = jnp.concatenate([even[j * side : (j + 1) * side], odd[j * side : (j + 1) * side]])
                tile_ref[pl.ds(pl.multiple_of(source * tall, tall), tall), pl.ds(lane * SIDE, SIDE)] = both.astype(
                    tile_ref.dtype
                )
    half = mm(tile_ref[...], left_ref[...]).astype(jnp.bfloat16)
    strips = []
    for j in range(2):
        goal = lax.rem(plane + shift_of(me, j) + 2 * planes, planes)
        strips.append(right_ref[pl.ds(pl.multiple_of(goal * tall, tall), tall), :])
    product = mm(jnp.concatenate(strips, axis=0), half).astype(piece_ref.dtype)
    for j in range(2):
        piece_ref[j] = product[j * tall : (j + 1) * tall]


def place_kernel(coord_ref, every_ref, out_ref):
    plane, first = coord_ref[1], pl.program_id(0) * (out_ref.shape[0] // 2)
    planes = every_ref.shape[0]
    groups, half = planes // 2, every_ref.shape[1] // 2
    for p in range(out_ref.shape[0] // 2):
        turn = lax.rem(plane - first - p + groups // 2 + 2 * planes, planes)
        d, far = lax.rem(turn, groups), turn >= groups
        for core in range(2):
            block = every_ref[2 * d + core].astype(jnp.float32)
            out_ref[2 * p + core] = jnp.where(far, block[half:], block[:half])


def shift_of(d, j):
    return d - 8 if j == 0 else d + 8


def spread(near, far, groups):
    landed = jnp.concatenate([near, far], axis=1)
    landed = jnp.broadcast_to(landed[None], (groups,) + landed.shape)
    landed = landed.reshape((-1,) + landed.shape[2:])
    return lax.all_to_all(landed, ("dp", "core"), split_axis=0, concat_axis=0, tiled=True)


def carry(value, tiles, groups, planes, shift):
    pairs = [
        (d * tiles + 2 * p + c, d * tiles + 2 * ((p + shift(d)) % planes) + c)
        for d in range(groups)
        for p in range(planes)
        for c in range(2)
    ]
    return lax.ppermute(value, ("dp", "z", "core"), pairs)


def body(acts, outgrads, grad, owners):
    width = acts.shape[2]
    groups = lax.axis_size("dp")
    planes = lax.axis_size("z")
    tiles = 2 * planes
    total_tokens = acts.shape[1] * groups
    me, plane, core = lax.axis_index("dp"), lax.axis_index("z"), lax.axis_index("core")
    coords = jnp.stack([me, plane])
    vmem = pl.BlockSpec(memory_space=pltpu.VMEM)
    smem = pl.BlockSpec(memory_space=pltpu.SMEM)
    params = pltpu.CompilerParams(vmem_limit_bytes=LIMIT)
    rows = 2 * len(blocks(width)) * SIDE

    turned = jnp.transpose(grad, (0, 2, 1))
    shards = turned.shape[1]
    near, far = (
        lax.dynamic_slice(
            turned, (2 * lax.rem(plane + shift_of(me, j) + 2 * planes, planes), 0, 0), (2, shards, width)
        )
        for j in range(2)
    )
    packed = pl.pallas_call(
        gram_kernel,
        out_shape=jax.ShapeDtypeStruct((rows, SIDE), jnp.bfloat16),
        in_specs=[pl.BlockSpec(memory_space=pl.ANY)] * 2,
        out_specs=vmem,
        scratch_shapes=[pltpu.VMEM((2,) + acts.shape[1:], acts.dtype), pltpu.SemaphoreType.DMA((2, 2))],
        compiler_params=pltpu.CompilerParams(vmem_limit_bytes=60 * 1024 * 1024),
        name="gram",
    )(acts, outgrads)
    parts = lax.all_to_all(
        packed.reshape(2 * groups, rows // groups // 2, SIDE), ("dp", "core"), split_axis=0, concat_axis=0, tiled=True
    )
    near, far = (
        carry(sent, tiles, groups, planes, functools.partial(shift_of, j=j)) for j, sent in enumerate((near, far))
    )
    landed = jnp.concatenate([near, far], axis=1)
    copies = pl.pallas_call(
        functools.partial(sum_kernel, total_tokens),
        out_shape=jax.ShapeDtypeStruct(
            (2 * groups, rows // groups // 2 + 2 * shards * width // SIDE, SIDE), jnp.bfloat16
        ),
        in_specs=[vmem, vmem],
        out_specs=vmem,
        compiler_params=params,
        name="sum",
    )(parts, landed)
    mixed = lax.all_to_all(copies, ("dp", "core"), split_axis=0, concat_axis=0, tiled=True)
    left_root, right_root, piece = pl.pallas_call(
        root_kernel,
        out_shape=(
            jax.ShapeDtypeStruct((width, width), jnp.float32),
            jax.ShapeDtypeStruct((width, width), jnp.float32),
            jax.ShapeDtypeStruct((2, 2 * shards, width), jnp.bfloat16),
        ),
        in_specs=[smem, vmem],
        out_specs=(vmem, vmem, vmem),
        scratch_shapes=[pltpu.VMEM((width, width), jnp.float32), pltpu.VMEM((width, width), jnp.bfloat16)],
        compiler_params=params,
        name="roots",
    )(coords, mixed)
    kept = jnp.stack(
        [jnp.where(owners[0, which] == me, root, 0.0) for which, root in enumerate((left_root, right_root))]
    )[None, None]

    landed = [
        carry(piece[j].reshape(2, shards, width), tiles, groups, planes, functools.partial(shift_of, j=j))
        for j in range(2)
    ]
    every = spread(*landed, groups)
    placed = pl.pallas_call(
        place_kernel,
        out_shape=jax.ShapeDtypeStruct((tiles, shards, width), jnp.float32),
        grid=(4,),
        in_specs=[smem, vmem],
        out_specs=pl.BlockSpec((tiles // 4, shards, width), lambda part: (part, 0, 0)),
        compiler_params=params,
        name="place",
    )(coords, every)
    return (kept, jnp.transpose(placed, (0, 2, 1)))


def solution(mesh):
    split = Mesh(mesh.devices.reshape(mesh.shape["dp"], -1, 2), ("dp", "z", "core"))
    mp = ("z", "core")
    in_specs = (P(mp, "dp", None), P(mp, "dp", None), P(None, None, mp), P(mp, None))
    out_specs = (P("dp", mp, None, None, None), P(None, None, mp))
    return jax.shard_map(body, mesh=split, in_specs=in_specs, out_specs=out_specs, check_vma=False)
```

```python
import functools

import jax
import jax.numpy as jnp
from jax import lax
from jax.experimental import pallas as pl
from jax.experimental.pallas import tpu as pltpu
from jax.sharding import Mesh, PartitionSpec as P

damping = 0.001
SIDE = 128
LIMIT = 48 * 1024 * 1024


def blocks(width):
    n = width // SIDE
    return [(i, j) for i in range(n) for j in range(i, n)]


def gram_kernel(acts_ref, outs_ref, packed_ref, held_ref, sems):
    tokens, width = acts_ref.shape[1:]
    places = blocks(width)
    wide = 2 * SIDE
    copies = []
    for which, ref in enumerate((acts_ref, outs_ref)):
        for part in range(2):
            span = pl.ds(part * (tokens // 2), tokens // 2)
            copies.append(pltpu.make_async_copy(ref.at[0, span], held_ref.at[which, span], sems.at[which, part]))
            copies[-1].start()
    for which in range(2):
        base = which * len(places)
        copies[2 * which].wait()
        copies[2 * which + 1].wait()
        for i in range(0, width, wide):
            left = held_ref[which, :, i : i + wide]
            part = lax.dot_general(
                left, held_ref[which, :, i:], (((0,), (0,)), ((), ())), preferred_element_type=jnp.float32
            )
            for spot, (r, c) in enumerate(places):
                if i <= r * SIDE < i + wide:
                    row, col = r * SIDE - i, c * SIDE - i
                    packed_ref[pl.ds((base + spot) * SIDE, SIDE), :] = part[
                        row : row + SIDE, col : col + SIDE
                    ].astype(packed_ref.dtype)


def sum_kernel(total_tokens, parts_ref, shards_ref, copies_ref):
    count, rows = parts_ref.shape[:2]
    tall, width = shards_ref.shape[1:]
    for tile in range(2):
        total = parts_ref[tile].astype(jnp.float32)
        for g in range(2 + tile, count, 2):
            total = total + parts_ref[g].astype(jnp.float32)
        total = (total / total_tokens).astype(copies_ref.dtype)
        for g in range(tile, count, 2):
            copies_ref[g, :rows] = total
            for lane in range(width // SIDE):
                copies_ref[g, pl.ds(rows + lane * tall, tall)] = shards_ref[tile, :, lane * SIDE : (lane + 1) * SIDE]


def mm(a, b):
    return jnp.dot(a.astype(jnp.bfloat16), b.astype(jnp.bfloat16), preferred_element_type=jnp.float32)


def diag(width):
    rows = lax.broadcasted_iota(jnp.int32, (width, width), 0)
    cols = lax.broadcasted_iota(jnp.int32, (width, width), 1)
    return rows == cols


def root_kernel(coord_ref, mixed_ref, left_ref, right_ref, piece_ref, stat_ref, tile_ref):
    width = stat_ref.shape[0]
    places = blocks(width)
    on_diag = diag(width)
    for which, root_ref in enumerate((left_ref, right_ref)):
        base = which * len(places)
        share = 2 * len(places) * SIDE // mixed_ref.shape[0]
        for spot, (r, c) in enumerate(places):
            start, stop, pieces = (base + spot) * SIDE, (base + spot + 1) * SIDE, []
            while start < stop:
                size = min(stop, (start // share + 1) * share) - start
                pieces.append(mixed_ref[start // share, pl.ds(start % share, size)])
                start += size
            block = jnp.concatenate(pieces, axis=0).astype(jnp.float32)
            stat_ref[pl.ds(r * SIDE, SIDE), pl.ds(c * SIDE, SIDE)] = block
            if r != c:
                stat_ref[pl.ds(c * SIDE, SIDE), pl.ds(r * SIDE, SIDE)] = block.T
        stat = stat_ref[...] + jnp.where(on_diag, damping, 0.0)
        squares = jnp.sum(jnp.sum(stat * stat, axis=0, keepdims=True), axis=1, keepdims=True)
        inv_scale = 1.0 / jnp.sqrt(squares)
        matrix = stat * inv_scale
        low = matrix.astype(jnp.bfloat16)
        square = mm(low, low)
        shift = square * 0.0625 - matrix * 0.625
        shift_low = shift.astype(jnp.bfloat16)
        quart = mm(shift_low, shift_low) + 3.125 * shift + jnp.where(on_diag, 625.0 / 256.0, 0.0)
        lead = matrix * 1.25 - square * 0.25
        tail = mm(lead, quart)
        factor = jnp.sqrt(jnp.sqrt(inv_scale))
        root_ref[...] = factor * (jnp.where(on_diag, 1.5625, 0.0) - 0.3125 * matrix - 0.25 * tail)

    me, plane, my_core = coord_ref[0], coord_ref[1], coord_ref[2]
    planes, tall = mixed_ref.shape[0], 16
    side = tall // 2
    for shift in range(planes):
        source = pl.multiple_of(lax.rem(plane - shift + planes, planes) * tall, tall)
        for lane in range(width // SIDE):
            both = []
            for core in range(2):
                d, j = holder_of(shift, core)
                rows = mixed_ref[2 * d + core, pl.ds(share + lane * tall, tall)].astype(jnp.float32)
                both.append(rows[j * side : (j + 1) * side])
            tile_ref[pl.ds(source, tall), pl.ds(lane * SIDE, SIDE)] = jnp.concatenate(both).astype(tile_ref.dtype)
    half = mm(tile_ref[...], left_ref[...]).astype(jnp.bfloat16)
    strips = []
    for j in range(2):
        goal = lax.rem(plane + shift_of(me, my_core, j) + 2 * planes, planes)
        strips.append(right_ref[pl.ds(pl.multiple_of(goal * tall, tall), tall), :])
    product = mm(jnp.concatenate(strips, axis=0), half).astype(piece_ref.dtype)
    for j in range(2):
        piece_ref[j] = product[j * tall : (j + 1) * tall]


def place_kernel(coord_ref, every_ref, out_ref):
    plane = coord_ref[1]
    planes = every_ref.shape[0]
    half = every_ref.shape[1] // 2
    for i in range(planes):
        block = every_ref[i].astype(jnp.float32)
        for j in range(2):
            source = lax.rem(plane - shift_of(i // 2, i % 2, j) + 2 * planes, planes)
            out_ref[2 * source + i % 2] = block[j * half : (j + 1) * half]


def shift_of(d, core, j):
    ahead = d + 8 if j == 0 else d - 8
    return ahead * (1 - 2 * core)


def holder_of(shift, core):
    turn = ((1 - 2 * core) * shift + 8) % 32
    return turn % 16, 1 - turn // 16


def spread(far, near, groups):
    landed = jnp.concatenate([far, near], axis=1)
    landed = jnp.broadcast_to(landed[None], (groups,) + landed.shape)
    landed = landed.reshape((-1,) + landed.shape[2:])
    return lax.all_to_all(landed, ("dp", "core"), split_axis=0, concat_axis=0, tiled=True)


def carry(value, tiles, groups, planes, shift):
    pairs = [
        (d * tiles + 2 * p + c, d * tiles + 2 * ((p + shift(d, c)) % planes) + c)
        for d in range(groups)
        for p in range(planes)
        for c in range(2)
    ]
    return lax.ppermute(value, ("dp", "z", "core"), pairs)


def body(acts, outgrads, grad, owners):
    width = acts.shape[2]
    groups = lax.axis_size("dp")
    planes = lax.axis_size("z")
    tiles = 2 * planes
    total_tokens = acts.shape[1] * groups
    me, plane, core = lax.axis_index("dp"), lax.axis_index("z"), lax.axis_index("core")
    coords = jnp.stack([me, plane, core])
    vmem = pl.BlockSpec(memory_space=pltpu.VMEM)
    smem = pl.BlockSpec(memory_space=pltpu.SMEM)
    params = pltpu.CompilerParams(vmem_limit_bytes=LIMIT)
    rows = 2 * len(blocks(width)) * SIDE

    turned = jnp.transpose(grad, (0, 2, 1))
    shards = turned.shape[1]
    far, near = (
        lax.dynamic_slice(
            turned, (2 * lax.rem(plane + shift_of(me, core, j) + 2 * planes, planes), 0, 0), (2, shards, width)
        )
        for j in range(2)
    )
    packed = pl.pallas_call(
        gram_kernel,
        out_shape=jax.ShapeDtypeStruct((rows, SIDE), jnp.bfloat16),
        in_specs=[pl.BlockSpec(memory_space=pl.ANY)] * 2,
        out_specs=vmem,
        scratch_shapes=[pltpu.VMEM((2,) + acts.shape[1:], acts.dtype), pltpu.SemaphoreType.DMA((2, 2))],
        compiler_params=pltpu.CompilerParams(vmem_limit_bytes=60 * 1024 * 1024),
        name="gram",
    )(acts, outgrads)
    parts = lax.all_to_all(
        packed.reshape(2 * groups, rows // groups // 2, SIDE), ("dp", "core"), split_axis=0, concat_axis=0, tiled=True
    )
    far, near = (
        carry(sent, tiles, groups, planes, functools.partial(shift_of, j=j)) for j, sent in enumerate((far, near))
    )
    landed = jnp.concatenate([far, near], axis=1)
    copies = pl.pallas_call(
        functools.partial(sum_kernel, total_tokens),
        out_shape=jax.ShapeDtypeStruct(
            (2 * groups, rows // groups // 2 + 2 * shards * width // SIDE, SIDE), jnp.bfloat16
        ),
        in_specs=[vmem, vmem],
        out_specs=vmem,
        compiler_params=params,
        name="sum",
    )(parts, landed)
    mixed = lax.all_to_all(copies, ("dp", "core"), split_axis=0, concat_axis=0, tiled=True)
    left_root, right_root, piece = pl.pallas_call(
        root_kernel,
        out_shape=(
            jax.ShapeDtypeStruct((width, width), jnp.float32),
            jax.ShapeDtypeStruct((width, width), jnp.float32),
            jax.ShapeDtypeStruct((2, 2 * shards, width), jnp.bfloat16),
        ),
        in_specs=[smem, vmem],
        out_specs=(vmem, vmem, vmem),
        scratch_shapes=[pltpu.VMEM((width, width), jnp.float32), pltpu.VMEM((width, width), jnp.bfloat16)],
        compiler_params=params,
        name="roots",
    )(coords, mixed)
    kept = jnp.stack(
        [jnp.where(owners[0, which] == me, root, 0.0) for which, root in enumerate((left_root, right_root))]
    )[None, None]

    landed = [
        carry(piece[j].reshape(2, shards, width), tiles, groups, planes, functools.partial(shift_of, j=j))
        for j in range(2)
    ]
    every = spread(*landed, groups)
    placed = pl.pallas_call(
        place_kernel,
        out_shape=jax.ShapeDtypeStruct((tiles, shards, width), jnp.float32),
        in_specs=[smem, vmem],
        out_specs=vmem,
        compiler_params=params,
        name="place",
    )(coords, every)
    return (kept, jnp.transpose(placed, (0, 2, 1)))


def solution(mesh):
    split = Mesh(mesh.devices.reshape(mesh.shape["dp"], -1, 2), ("dp", "z", "core"))
    mp = ("z", "core")
    in_specs = (P(mp, "dp", None), P(mp, "dp", None), P(None, None, mp), P(mp, None))
    out_specs = (P("dp", mp, None, None, None), P(None, None, mp))
    return jax.shard_map(body, mesh=split, in_specs=in_specs, out_specs=out_specs, check_vma=False)
```

```python
import functools

import jax
import jax.numpy as jnp
from jax import lax
from jax.experimental import pallas as pl
from jax.experimental.pallas import tpu as pltpu
from jax.sharding import Mesh, PartitionSpec as P

damping = 0.001
SIDE = 128
LIMIT = 48 * 1024 * 1024


def blocks(width):
    n = width // SIDE
    return [(i, j) for i in range(n) for j in range(i, n)]


def gram_kernel(coord_ref, acts_ref, outs_ref, grad_ref, packed_ref, far_ref, near_ref, held_ref, sems, grad_sems):
    tokens, width = acts_ref.shape[1:]
    places = blocks(width)
    wide = 2 * SIDE
    copies = []
    for which, ref in enumerate((acts_ref, outs_ref)):
        for part in range(2):
            span = pl.ds(part * (tokens // 2), tokens // 2)
            copies.append(pltpu.make_async_copy(ref.at[0, span], held_ref.at[which, span], sems.at[which, part]))
            copies[-1].start()
    me, plane, core = coord_ref[0], coord_ref[1], coord_ref[2]
    planes = grad_ref.shape[0] // 2
    shards = []
    for j, ref in enumerate((far_ref, near_ref)):
        goal = lax.rem(plane + shift_of(me, core, j) + 2 * planes, planes)
        shards.append(pltpu.make_async_copy(grad_ref.at[pl.ds(2 * goal, 2)], ref, grad_sems.at[j]))
        shards[-1].start()
    for which in range(2):
        base = which * len(places)
        copies[2 * which].wait()
        copies[2 * which + 1].wait()
        for i in range(0, width, wide):
            left = held_ref[which, :, i : i + wide]
            part = lax.dot_general(
                left, held_ref[which, :, i:], (((0,), (0,)), ((), ())), preferred_element_type=jnp.float32
            )
            for spot, (r, c) in enumerate(places):
                if i <= r * SIDE < i + wide:
                    row, col = r * SIDE - i, c * SIDE - i
                    packed_ref[pl.ds((base + spot) * SIDE, SIDE), :] = part[
                        row : row + SIDE, col : col + SIDE
                    ].astype(packed_ref.dtype)
    for copy in shards:
        copy.wait()


def sum_kernel(total_tokens, parts_ref, shards_ref, copies_ref):
    count, rows = parts_ref.shape[:2]
    tall, width = shards_ref.shape[1:]
    for tile in range(2):
        total = parts_ref[tile].astype(jnp.float32)
        for g in range(2 + tile, count, 2):
            total = total + parts_ref[g].astype(jnp.float32)
        total = (total / total_tokens).astype(copies_ref.dtype)
        for g in range(tile, count, 2):
            copies_ref[g, :rows] = total
            for lane in range(width // SIDE):
                copies_ref[g, pl.ds(rows + lane * tall, tall)] = shards_ref[tile, :, lane * SIDE : (lane + 1) * SIDE]


def mm(a, b):
    return jnp.dot(a.astype(jnp.bfloat16), b.astype(jnp.bfloat16), preferred_element_type=jnp.float32)


def diag(width):
    rows = lax.broadcasted_iota(jnp.int32, (width, width), 0)
    cols = lax.broadcasted_iota(jnp.int32, (width, width), 1)
    return rows == cols


def root_kernel(coord_ref, mixed_ref, left_ref, right_ref, piece_ref, stat_ref, tile_ref):
    width = stat_ref.shape[0]
    places = blocks(width)
    on_diag = diag(width)
    for which, root_ref in enumerate((left_ref, right_ref)):
        base = which * len(places)
        share = 2 * len(places) * SIDE // mixed_ref.shape[0]
        for spot, (r, c) in enumerate(places):
            start, stop, pieces = (base + spot) * SIDE, (base + spot + 1) * SIDE, []
            while start < stop:
                size = min(stop, (start // share + 1) * share) - start
                pieces.append(mixed_ref[start // share, pl.ds(start % share, size)])
                start += size
            block = jnp.concatenate(pieces, axis=0).astype(jnp.float32)
            stat_ref[pl.ds(r * SIDE, SIDE), pl.ds(c * SIDE, SIDE)] = block
            if r != c:
                stat_ref[pl.ds(c * SIDE, SIDE), pl.ds(r * SIDE, SIDE)] = block.T
        stat = stat_ref[...] + jnp.where(on_diag, damping, 0.0)
        squares = jnp.sum(jnp.sum(stat * stat, axis=0, keepdims=True), axis=1, keepdims=True)
        inv_scale = 1.0 / jnp.sqrt(squares)
        matrix = stat * inv_scale
        low = matrix.astype(jnp.bfloat16)
        square = mm(low, low)
        shift = square * 0.0625 - matrix * 0.625
        shift_low = shift.astype(jnp.bfloat16)
        quart = mm(shift_low, shift_low) + 3.125 * shift + jnp.where(on_diag, 625.0 / 256.0, 0.0)
        lead = matrix * 1.25 - square * 0.25
        tail = mm(lead, quart)
        factor = jnp.sqrt(jnp.sqrt(inv_scale))
        root_ref[...] = factor * (jnp.where(on_diag, 1.5625, 0.0) - 0.3125 * matrix - 0.25 * tail)

    me, plane, my_core = coord_ref[0], coord_ref[1], coord_ref[2]
    planes, tall = mixed_ref.shape[0], 16
    side = tall // 2
    for shift in range(planes):
        source = pl.multiple_of(lax.rem(plane - shift + planes, planes) * tall, tall)
        for lane in range(width // SIDE):
            both = []
            for core in range(2):
                d, j = holder_of(shift, core)
                rows = mixed_ref[2 * d + core, pl.ds(share + lane * tall, tall)].astype(jnp.float32)
                both.append(rows[j * side : (j + 1) * side])
            tile_ref[pl.ds(source, tall), pl.ds(lane * SIDE, SIDE)] = jnp.concatenate(both).astype(tile_ref.dtype)
    half = mm(tile_ref[...], left_ref[...]).astype(jnp.bfloat16)
    strips = []
    for j in range(2):
        goal = lax.rem(plane + shift_of(me, my_core, j) + 2 * planes, planes)
        strips.append(right_ref[pl.ds(pl.multiple_of(goal * tall, tall), tall), :])
    product = mm(jnp.concatenate(strips, axis=0), half).astype(piece_ref.dtype)
    for j in range(2):
        piece_ref[j] = product[j * tall : (j + 1) * tall]


def place_kernel(coord_ref, every_ref, out_ref, held_ref, sem):
    plane = coord_ref[1]
    planes = every_ref.shape[0]
    half = every_ref.shape[1] // 2
    for shift in range(planes):
        source = lax.rem(plane - shift + planes, planes)
        for core in range(2):
            d, j = holder_of(shift, core)
            block = every_ref[2 * d + core].astype(jnp.float32)
            held_ref[2 * source + core] = block[j * half : (j + 1) * half]
        span = pl.ds(2 * source, 2)
        pltpu.make_async_copy(held_ref.at[span], out_ref.at[span], sem).start()
    pltpu.make_async_copy(held_ref, out_ref, sem).wait()


def seat_of(d, core):
    return d + core * (d % 8 == 0) * (8 - 2 * d)


def shift_of(d, core, j):
    seat = seat_of(d, core)
    return (seat + 8 if j == 0 else seat - 8) * (1 - 2 * core)


def holder_of(shift, core):
    turn = ((1 - 2 * core) * shift + 8) % 32
    return seat_of(turn % 16, core), 1 - turn // 16


def spread(far, near, groups):
    landed = jnp.concatenate([far, near], axis=1)
    landed = jnp.broadcast_to(landed[None], (groups,) + landed.shape)
    landed = landed.reshape((-1,) + landed.shape[2:])
    return lax.all_to_all(landed, ("dp", "core"), split_axis=0, concat_axis=0, tiled=True)


def carry(value, tiles, groups, planes, shift):
    pairs = [
        (d * tiles + 2 * p + c, d * tiles + 2 * ((p + shift(d, c)) % planes) + c)
        for d in range(groups)
        for p in range(planes)
        for c in range(2)
    ]
    return lax.ppermute(value, ("dp", "z", "core"), pairs)


def body(acts, outgrads, grad, owners):
    width = acts.shape[2]
    groups = lax.axis_size("dp")
    planes = lax.axis_size("z")
    tiles = 2 * planes
    total_tokens = acts.shape[1] * groups
    me, plane, core = lax.axis_index("dp"), lax.axis_index("z"), lax.axis_index("core")
    coords = jnp.stack([me, plane, core])
    vmem = pl.BlockSpec(memory_space=pltpu.VMEM)
    smem = pl.BlockSpec(memory_space=pltpu.SMEM)
    params = pltpu.CompilerParams(vmem_limit_bytes=LIMIT)
    rows = 2 * len(blocks(width)) * SIDE

    turned = jnp.transpose(grad, (0, 2, 1))
    shards = turned.shape[1]
    shard = jax.ShapeDtypeStruct((2, shards, width), grad.dtype)
    packed, far, near = pl.pallas_call(
        gram_kernel,
        out_shape=(jax.ShapeDtypeStruct((rows, SIDE), jnp.bfloat16), shard, shard),
        in_specs=[smem] + [pl.BlockSpec(memory_space=pl.ANY)] * 3,
        out_specs=(vmem, vmem, vmem),
        scratch_shapes=[
            pltpu.VMEM((2,) + acts.shape[1:], acts.dtype),
            pltpu.SemaphoreType.DMA((2, 2)),
            pltpu.SemaphoreType.DMA((2,)),
        ],
        compiler_params=pltpu.CompilerParams(vmem_limit_bytes=60 * 1024 * 1024),
        name="gram",
    )(coords, acts, outgrads, turned)
    parts = lax.all_to_all(
        packed.reshape(2 * groups, rows // groups // 2, SIDE), ("dp", "core"), split_axis=0, concat_axis=0, tiled=True
    )
    far, near = (
        carry(sent, tiles, groups, planes, functools.partial(shift_of, j=j)) for j, sent in enumerate((far, near))
    )
    landed = jnp.concatenate([far, near], axis=1)
    copies = pl.pallas_call(
        functools.partial(sum_kernel, total_tokens),
        out_shape=jax.ShapeDtypeStruct(
            (2 * groups, rows // groups // 2 + 2 * shards * width // SIDE, SIDE), jnp.bfloat16
        ),
        in_specs=[vmem, vmem],
        out_specs=vmem,
        compiler_params=params,
        name="sum",
    )(parts, landed)
    mixed = lax.all_to_all(copies, ("dp", "core"), split_axis=0, concat_axis=0, tiled=True)
    left_root, right_root, piece = pl.pallas_call(
        root_kernel,
        out_shape=(
            jax.ShapeDtypeStruct((width, width), jnp.float32),
            jax.ShapeDtypeStruct((width, width), jnp.float32),
            jax.ShapeDtypeStruct((2, 2 * shards, width), jnp.bfloat16),
        ),
        in_specs=[smem, vmem],
        out_specs=(vmem, vmem, vmem),
        scratch_shapes=[pltpu.VMEM((width, width), jnp.float32), pltpu.VMEM((width, width), jnp.bfloat16)],
        compiler_params=params,
        name="roots",
    )(coords, mixed)
    kept = jnp.stack(
        [jnp.where(owners[0, which] == me, root, 0.0) for which, root in enumerate((left_root, right_root))]
    )[None, None]

    landed = [
        carry(piece[j].reshape(2, shards, width), tiles, groups, planes, functools.partial(shift_of, j=j))
        for j in range(2)
    ]
    every = spread(*landed, groups)
    placed = pl.pallas_call(
        place_kernel,
        out_shape=jax.ShapeDtypeStruct((tiles, shards, width), jnp.float32),
        in_specs=[smem, vmem],
        out_specs=pl.BlockSpec(memory_space=pl.ANY),
        scratch_shapes=[pltpu.VMEM((tiles, shards, width), jnp.float32), pltpu.SemaphoreType.DMA],
        compiler_params=params,
        name="place",
    )(coords, every)
    return (kept, jnp.transpose(placed, (0, 2, 1)))


def solution(mesh):
    split = Mesh(mesh.devices.reshape(mesh.shape["dp"], -1, 2), ("dp", "z", "core"))
    mp = ("z", "core")
    in_specs = (P(mp, "dp", None), P(mp, "dp", None), P(None, None, mp), P(mp, None))
    out_specs = (P("dp", mp, None, None, None), P(None, None, mp))
    return jax.shard_map(body, mesh=split, in_specs=in_specs, out_specs=out_specs, check_vma=False)
```

```python
import functools

import jax
import jax.numpy as jnp
from jax import lax
from jax.experimental import pallas as pl
from jax.experimental.pallas import tpu as pltpu
from jax.sharding import Mesh, PartitionSpec as P

damping = 0.001
SIDE = 128
LIMIT = 48 * 1024 * 1024


def blocks(width):
    n = width // SIDE
    return [(i, j) for i in range(n) for j in range(i, n)]


def gram_kernel(acts_ref, outs_ref, packed_ref, held_ref, sems):
    tokens, width = acts_ref.shape[1:]
    places = blocks(width)
    wide = 2 * SIDE
    copies = []
    for which, ref in enumerate((acts_ref, outs_ref)):
        for part in range(2):
            span = pl.ds(part * (tokens // 2), tokens // 2)
            copies.append(pltpu.make_async_copy(ref.at[0, span], held_ref.at[which, span], sems.at[which, part]))
            copies[-1].start()
    for which in range(2):
        base = which * len(places)
        copies[2 * which].wait()
        copies[2 * which + 1].wait()
        for i in range(0, width, wide):
            left = held_ref[which, :, i : i + wide]
            part = lax.dot_general(
                left, held_ref[which, :, i:], (((0,), (0,)), ((), ())), preferred_element_type=jnp.float32
            )
            for spot, (r, c) in enumerate(places):
                if i <= r * SIDE < i + wide:
                    row, col = r * SIDE - i, c * SIDE - i
                    packed_ref[pl.ds((base + spot) * SIDE, SIDE), :] = part[
                        row : row + SIDE, col : col + SIDE
                    ].astype(packed_ref.dtype)


def sum_kernel(total_tokens, parts_ref, shards_ref, copies_ref):
    count, rows = parts_ref.shape[:2]
    tall, width = shards_ref.shape[1:]
    for tile in range(2):
        total = parts_ref[tile].astype(jnp.float32)
        for g in range(2 + tile, count, 2):
            total = total + parts_ref[g].astype(jnp.float32)
        total = (total / total_tokens).astype(copies_ref.dtype)
        for g in range(tile, count, 2):
            copies_ref[g, :rows] = total
            for lane in range(width // SIDE):
                copies_ref[g, pl.ds(rows + lane * tall, tall)] = shards_ref[tile, :, lane * SIDE : (lane + 1) * SIDE]


def mm(a, b):
    return jnp.dot(a.astype(jnp.bfloat16), b.astype(jnp.bfloat16), preferred_element_type=jnp.float32)


def diag(width):
    rows = lax.broadcasted_iota(jnp.int32, (width, width), 0)
    cols = lax.broadcasted_iota(jnp.int32, (width, width), 1)
    return rows == cols


def root_kernel(coord_ref, mixed_ref, left_ref, right_ref, piece_ref, stat_ref, tile_ref):
    width = stat_ref.shape[0]
    places = blocks(width)
    on_diag = diag(width)
    for which, root_ref in enumerate((left_ref, right_ref)):
        base = which * len(places)
        share = 2 * len(places) * SIDE // mixed_ref.shape[0]
        for spot, (r, c) in enumerate(places):
            start, stop, pieces = (base + spot) * SIDE, (base + spot + 1) * SIDE, []
            while start < stop:
                size = min(stop, (start // share + 1) * share) - start
                pieces.append(mixed_ref[start // share, pl.ds(start % share, size)])
                start += size
            block = jnp.concatenate(pieces, axis=0).astype(jnp.float32)
            stat_ref[pl.ds(r * SIDE, SIDE), pl.ds(c * SIDE, SIDE)] = block
            if r != c:
                stat_ref[pl.ds(c * SIDE, SIDE), pl.ds(r * SIDE, SIDE)] = block.T
        stat = stat_ref[...] + jnp.where(on_diag, damping, 0.0)
        squares = jnp.sum(jnp.sum(stat * stat, axis=0, keepdims=True), axis=1, keepdims=True)
        inv_scale = 1.0 / jnp.sqrt(squares)
        matrix = stat * inv_scale
        low = matrix.astype(jnp.bfloat16)
        square = mm(low, low)
        shift = square * 0.0625 - matrix * 0.625
        shift_low = shift.astype(jnp.bfloat16)
        quart = mm(shift_low, shift_low) + 3.125 * shift + jnp.where(on_diag, 625.0 / 256.0, 0.0)
        lead = matrix * 1.25 - square * 0.25
        tail = mm(lead, quart)
        factor = jnp.sqrt(jnp.sqrt(inv_scale))
        root_ref[...] = factor * (jnp.where(on_diag, 1.5625, 0.0) - 0.3125 * matrix - 0.25 * tail)

    me, plane, my_core = coord_ref[0], coord_ref[1], coord_ref[2]
    planes, tall = mixed_ref.shape[0], 16
    side = tall // 2
    for shift in range(planes):
        source = pl.multiple_of(lax.rem(plane - shift + planes, planes) * tall, tall)
        for lane in range(width // SIDE):
            both = []
            for core in range(2):
                d, j = holder_of(shift, core)
                rows = mixed_ref[2 * d + core, pl.ds(share + lane * tall, tall)].astype(jnp.float32)
                both.append(rows[j * side : (j + 1) * side])
            tile_ref[pl.ds(source, tall), pl.ds(lane * SIDE, SIDE)] = jnp.concatenate(both).astype(tile_ref.dtype)
    half = mm(tile_ref[...], left_ref[...]).astype(jnp.bfloat16)
    strips = []
    for j in range(2):
        goal = lax.rem(plane + shift_of(me, my_core, j) + 2 * planes, planes)
        strips.append(right_ref[pl.ds(pl.multiple_of(goal * tall, tall), tall), :])
    product = mm(jnp.concatenate(strips, axis=0), half).astype(piece_ref.dtype)
    for j in range(2):
        piece_ref[j] = product[j * tall : (j + 1) * tall]


def place_kernel(coord_ref, every_ref, out_ref, held_ref, sem):
    plane = coord_ref[1]
    planes = every_ref.shape[0]
    half = every_ref.shape[1] // 2
    for shift in range(planes):
        source = lax.rem(plane - shift + planes, planes)
        for core in range(2):
            d, j = holder_of(shift, core)
            block = every_ref[2 * d + core].astype(jnp.float32)
            held_ref[2 * source + core] = block[j * half : (j + 1) * half]
        span = pl.ds(2 * source, 2)
        pltpu.make_async_copy(held_ref.at[span], out_ref.at[span], sem).start()
    pltpu.make_async_copy(held_ref, out_ref, sem).wait()


def seat_of(d, core):
    return d + core * (d % 8 == 0) * (8 - 2 * d)


def shift_of(d, core, j):
    seat = seat_of(d, core)
    return (seat + 8 if j == 0 else seat - 8) * (1 - 2 * core)


def holder_of(shift, core):
    turn = ((1 - 2 * core) * shift + 8) % 32
    return seat_of(turn % 16, core), 1 - turn // 16


def fan_kernel(landed_ref, copies_ref):
    for g in range(copies_ref.shape[0]):
        copies_ref[g] = landed_ref[g % 2]


def spread(far, near, groups, params):
    landed = jnp.concatenate([far, near], axis=1)
    vmem = pl.BlockSpec(memory_space=pltpu.VMEM)
    copies = pl.pallas_call(
        fan_kernel,
        out_shape=jax.ShapeDtypeStruct((2 * groups,) + landed.shape[1:], landed.dtype),
        in_specs=[vmem],
        out_specs=vmem,
        compiler_params=params,
        name="fan",
    )(landed)
    return lax.all_to_all(copies, ("dp", "core"), split_axis=0, concat_axis=0, tiled=True)


def carry(value, tiles, groups, planes, shift):
    pairs = [
        (d * tiles + 2 * p + c, d * tiles + 2 * ((p + shift(d, c)) % planes) + c)
        for d in range(groups)
        for p in range(planes)
        for c in range(2)
    ]
    return lax.ppermute(value, ("dp", "z", "core"), pairs)


def body(acts, outgrads, grad, owners):
    width = acts.shape[2]
    groups = lax.axis_size("dp")
    planes = lax.axis_size("z")
    tiles = 2 * planes
    total_tokens = acts.shape[1] * groups
    me, plane, core = lax.axis_index("dp"), lax.axis_index("z"), lax.axis_index("core")
    coords = jnp.stack([me, plane, core])
    vmem = pl.BlockSpec(memory_space=pltpu.VMEM)
    smem = pl.BlockSpec(memory_space=pltpu.SMEM)
    params = pltpu.CompilerParams(vmem_limit_bytes=LIMIT)
    rows = 2 * len(blocks(width)) * SIDE

    turned = jnp.transpose(grad, (0, 2, 1))
    shards = turned.shape[1]
    far, near = (
        lax.dynamic_slice(
            turned, (2 * lax.rem(plane + shift_of(me, core, j) + 2 * planes, planes), 0, 0), (2, shards, width)
        )
        for j in range(2)
    )
    packed = pl.pallas_call(
        gram_kernel,
        out_shape=jax.ShapeDtypeStruct((rows, SIDE), jnp.bfloat16),
        in_specs=[pl.BlockSpec(memory_space=pl.ANY)] * 2,
        out_specs=vmem,
        scratch_shapes=[pltpu.VMEM((2,) + acts.shape[1:], acts.dtype), pltpu.SemaphoreType.DMA((2, 2))],
        compiler_params=pltpu.CompilerParams(vmem_limit_bytes=60 * 1024 * 1024),
        name="gram",
    )(acts, outgrads)
    parts = lax.all_to_all(
        packed.reshape(2 * groups, rows // groups // 2, SIDE), ("dp", "core"), split_axis=0, concat_axis=0, tiled=True
    )
    far, near = (
        carry(sent, tiles, groups, planes, functools.partial(shift_of, j=j)) for j, sent in enumerate((far, near))
    )
    landed = jnp.concatenate([far, near], axis=1)
    copies = pl.pallas_call(
        functools.partial(sum_kernel, total_tokens),
        out_shape=jax.ShapeDtypeStruct(
            (2 * groups, rows // groups // 2 + 2 * shards * width // SIDE, SIDE), jnp.bfloat16
        ),
        in_specs=[vmem, vmem],
        out_specs=vmem,
        compiler_params=params,
        name="sum",
    )(parts, landed)
    mixed = lax.all_to_all(copies, ("dp", "core"), split_axis=0, concat_axis=0, tiled=True)
    left_root, right_root, piece = pl.pallas_call(
        root_kernel,
        out_shape=(
            jax.ShapeDtypeStruct((width, width), jnp.float32),
            jax.ShapeDtypeStruct((width, width), jnp.float32),
            jax.ShapeDtypeStruct((2, 2 * shards, width), jnp.bfloat16),
        ),
        in_specs=[smem, vmem],
        out_specs=(vmem, vmem, vmem),
        scratch_shapes=[pltpu.VMEM((width, width), jnp.float32), pltpu.VMEM((width, width), jnp.bfloat16)],
        compiler_params=params,
        name="roots",
    )(coords, mixed)
    kept = jnp.stack(
        [jnp.where(owners[0, which] == me, root, 0.0) for which, root in enumerate((left_root, right_root))]
    )[None, None]

    landed = [
        carry(piece[j].reshape(2, shards, width), tiles, groups, planes, functools.partial(shift_of, j=j))
        for j in range(2)
    ]
    every = spread(*landed, groups, params)
    placed = pl.pallas_call(
        place_kernel,
        out_shape=jax.ShapeDtypeStruct((tiles, shards, width), jnp.float32),
        in_specs=[smem, vmem],
        out_specs=pl.BlockSpec(memory_space=pl.ANY),
        scratch_shapes=[pltpu.VMEM((tiles, shards, width), jnp.float32), pltpu.SemaphoreType.DMA],
        compiler_params=params,
        name="place",
    )(coords, every)
    return (kept, jnp.transpose(placed, (0, 2, 1)))


def solution(mesh):
    split = Mesh(mesh.devices.reshape(mesh.shape["dp"], -1, 2), ("dp", "z", "core"))
    mp = ("z", "core")
    in_specs = (P(mp, "dp", None), P(mp, "dp", None), P(None, None, mp), P(mp, None))
    out_specs = (P("dp", mp, None, None, None), P(None, None, mp))
    return jax.shard_map(body, mesh=split, in_specs=in_specs, out_specs=out_specs, check_vma=False)
```
